32 devices in a mesh: members: 2 (over y), lon: 8 (over z, x), lat: 2 (over core).
Axes of the slice: x: 2, y: 2, z: 4, core: 2. Of those that a mesh axis runs over, the one named last changes fastest.
Arguments:
- field: bfloat16 [256, 88, 384], P(('members', 'lat'), 'lon'), parts along dimension 0, may hold values from -6 to 6
- reach: int32 [128], P('lat'), may hold values from 1 to 2, as said below
- slot_rows: int32 [128, 16], P('lat'), may hold values from 0 to 6
- slot_cols: int32 [128, 16], P('lat'), may hold values from 0 to 3, as said below
- counts: int32 [128], P('lat'), may hold values from 4 to 16, as said below
- filters: bfloat16 [128, 16, 36], P('lat'), may hold values from -1 to 1
- mixing: bfloat16 [3456, 384], replicated, may hold values from -0.109375 to 0.109375
- bias: float32 [384], replicated, may hold values from -3 to 3
Outputs:
- activated: bfloat16 [256, 88, 384], P(('members', 'lat'), 'lon'), parts along dimension 0
The draws below stay inside these ranges and needn't reach their ends.
There are 2 independent parts, one for each index of `members`. The reference program is written for one: setup_inputs(seed, part) draws one part's arguments, and reference() takes and returns one part's arrays. A program takes and returns all parts, laid end to end along the dimension named above; an argument that names none is the same for every part. Nothing has to cross between parts.
Inputs may be any that keep to these rules, and one draw needn't show every extreme that they name: `reach`: the first row reaches 2 blocks. slot_cols[i, s] < 2 reach[i]; the live slots of a row name distinct pairs (slot_rows, slot_cols). `counts`: the first row has 16 live slots.
All inputs are finite; a program needn't handle non-finite values.
Results may differ from the reference program's by a relative error of at most 0.0047.
Values may be sent and summed in bfloat16 or wider, within the bound.
A program may use at most 64 MiB of HBM per device.

```python
import jax
import jax.numpy as jnp
from jax import lax

C = 384
BASIS = 9
RAD = 3
BLOCK = 4
REACH_MAX = 2
SLOTS = 16
LAT_ROWS = 128
LON = 88


def wide_reach(key):
    rows_here = jnp.arange(LAT_ROWS, dtype=jnp.int32)
    picks = jax.random.randint(jax.random.fold_in(key, 101), (LAT_ROWS,), 0, LAT_ROWS)
    return (1 + (REACH_MAX - 1) * (picks >= rows_here).astype(jnp.int32)).astype(jnp.int32)


def block_order(key):
    reach_rows = wide_reach(key)
    total_blocks = (2 * RAD + 1) * 2 * REACH_MAX
    row_keys = jax.random.split(jax.random.fold_in(key, 202), LAT_ROWS)
    scores = jax.vmap(lambda single: jax.random.permutation(single, total_blocks))(row_keys)
    block_ids = jnp.arange(total_blocks, dtype=jnp.int32)
    column_ids = block_ids % (2 * REACH_MAX)
    invalid = (column_ids[None, :] >= 2 * reach_rows[:, None]).astype(jnp.int32)
    order = jnp.argsort(scores.astype(jnp.int32) + total_blocks * invalid, axis=1, stable=True)[:, :SLOTS]
    order = order.astype(jnp.int32)
    source_rows = order // (2 * REACH_MAX)
    source_cols = order % (2 * REACH_MAX) % (2 * reach_rows[:, None])
    return (source_rows.astype(jnp.int32), source_cols.astype(jnp.int32))


def draw_reach(key, part):
    return wide_reach(key)


def draw_slot_rows(key, part):
    return block_order(key)[0]


def draw_slot_cols(key, part):
    return block_order(key)[1]


def draw_counts(key, part):
    reach_rows = wide_reach(key)
    key = jax.random.fold_in(key, 17)
    wide_rows = reach_rows == REACH_MAX
    lower = jnp.where(wide_rows, SLOTS // 2, SLOTS // 4)
    upper = jnp.where(wide_rows, SLOTS, SLOTS // 2)
    picks = jax.random.randint(key, (LAT_ROWS,), 0, SLOTS + 1)
    live_counts = lower + picks % (upper - lower + 1)
    live_counts = live_counts.at[0].set(SLOTS).at[LAT_ROWS - 1].set(SLOTS // 4)
    return live_counts.astype(jnp.int32)


def shard_levels(own_key, dims, shards, low, top_value):
    gain = 1.0
    for axis_at, blocks in shards:
        draws = jax.random.uniform(jax.random.fold_in(jax.random.fold_in(own_key, 6), axis_at), (blocks,), jnp.float32, low / len(shards), top_value / len(shards))
        gain = gain * jnp.repeat(jnp.exp(draws), dims[axis_at] // blocks).reshape((-1,) + (1,) * (len(dims) - 1 - axis_at))
    return gain


def gaussian(rng, dims, scale, bound, shards=(), held_as=jnp.bfloat16):
    result = jax.random.normal(rng, dims, jnp.float32) * scale
    if len(shards) > 0:
        result = shard_levels(rng, dims, shards, -0.22, 0.18) * result
    return jnp.clip(result, min=-bound, max=bound).astype(held_as)


def setup_inputs(seed: int = 0, part: int = 0) -> dict:
    streams_of = jax.random.split(jax.random.key(seed), 9)
    own_keys = jax.random.split(jax.random.fold_in(streams_of[8], part), 9)
    field = gaussian(own_keys[0], (LAT_ROWS, LON, C), 1.0, 6.0, ((0, 2), (1, 8)))
    reach = draw_reach(jax.random.fold_in(streams_of[8], 71), part)
    slot_rows = draw_slot_rows(jax.random.fold_in(streams_of[8], 71), part)
    slot_cols = draw_slot_cols(jax.random.fold_in(streams_of[8], 71), part)
    counts = draw_counts(jax.random.fold_in(streams_of[8], 71), part)
    filters = gaussian(streams_of[5], (LAT_ROWS, SLOTS, BASIS * BLOCK), (SLOTS * BLOCK // 2) ** -0.5, 1.0, ((0, 2),))
    mixing = gaussian(streams_of[6], (BASIS * C, C), (BASIS * C) ** -0.5, 0.109375)
    bias = gaussian(streams_of[7], (C,), 0.5, 3.0, (), jnp.float32)
    return {"field": field, "reach": reach, "slot_rows": slot_rows, "slot_cols": slot_cols, "counts": counts, "filters": filters, "mixing": mixing, "bias": bias}


def reference(field, reach, slot_rows, slot_cols, counts, filters, mixing, bias):
    window_rows = 2 * RAD + 1
    padded = jnp.pad(field, ((RAD, RAD), (0, 0), (0, 0)))

    def one_row(row_index):
        window = lax.dynamic_slice_in_dim(padded, row_index, window_rows, 0)

        def slot_step(slot_index, running):
            source_row = slot_rows[row_index, slot_index].astype(jnp.int32)
            source = lax.dynamic_index_in_dim(window, source_row, 0, keepdims=False).astype(jnp.float32)
            offset = (slot_cols[row_index, slot_index] - reach[row_index]) * BLOCK
            turned = jnp.roll(source, -offset, axis=0)
            longer = jnp.concatenate([turned, turned[:BLOCK]], axis=0)
            stacked = jnp.stack([longer[t:t + LON] for t in range(BLOCK)], axis=0)
            slot_taps = filters[row_index, slot_index].astype(jnp.float32).reshape(BASIS, BLOCK)
            return running + jnp.einsum("kt,tlc->lkc", slot_taps, stacked, precision=lax.Precision.HIGHEST)

        total = lax.fori_loop(0, counts[row_index], slot_step, jnp.zeros((LON, BASIS, C), jnp.float32))
        conv = total.astype(jnp.bfloat16).reshape(LON, BASIS * C)
        pre_act = jnp.dot(conv, mixing, preferred_element_type=jnp.float32) + bias
        return jax.nn.gelu(pre_act, approximate=False).astype(jnp.bfloat16)

    return lax.map(one_row, jnp.arange(LAT_ROWS, dtype=jnp.int32))
```

```python
import functools

import jax
import jax.numpy as jnp
from jax import lax
from jax.experimental import pallas as pl
from jax.experimental.pallas import tpu as pltpu
from jax.sharding import PartitionSpec as P

BASIS = 9
RAD = 3
BLOCK = 4
SLOTS = 16
HALO = 8
ROWS = 16
MESH = pl.DeviceIdType.MESH


def kernel(
    lon_size,
    x_ref,
    rows_ref,
    cols_ref,
    reach_ref,
    counts_ref,
    filt_ref,
    mix_ref,
    bias_ref,
    out_ref,
    ext,
    mix,
    hot,
    taps,
    near,
    far,
    conv,
    own_sem,
    mix_sem,
    pair_send,
    pair_recv,
    fwd_send,
    fwd_recv,
    lat_send,
    lat_recv,
):
    cols, rows, width = x_ref.shape
    chunks = rows // ROWS
    lon = lax.axis_index("lon")
    lat = lax.axis_index("lat")
    even = lax.rem(lon, 2) == 0
    partner = jnp.where(even, lon + 1, lon - 1)
    ahead = lax.rem(lon + 2, lon_size)
    behind = lax.rem(lon + lon_size - 2, lon_size)
    onward = jnp.where(even, ahead, behind)
    other = 1 - lat

    def chunk_at(step):
        return jnp.where(lat == 0, chunks - 1 - step, step)

    def rows_at(start):
        return pl.ds(pl.multiple_of(start, ROWS), ROWS)

    own_copy = pltpu.make_async_copy(
        x_ref, ext.at[pl.ds(cols, cols), pl.ds(ROWS, rows), :], own_sem
    )
    own_copy.start()
    mix_copy = pltpu.make_async_copy(mix_ref, mix, mix_sem)
    mix_copy.start()

    barrier = pltpu.get_barrier_semaphore()
    for target in ({"lon": partner}, {"lon": ahead}, {"lon": behind}, {"lat": other}):
        pl.semaphore_signal(barrier, inc=1, device_id=target, device_id_type=MESH)
    pl.semaphore_wait(barrier, 4)

    there = jnp.where(even, 0, 2 * cols)
    here = 2 * cols - there
    fwd_from = jnp.where(even, here + cols - HALO, here)
    fwd_to = jnp.where(even, cols - HALO, 2 * cols)

    def pair_copy(step):
        first = chunk_at(step) * ROWS
        return pltpu.make_async_remote_copy(
            src_ref=x_ref.at[:, rows_at(first), :],
            dst_ref=ext.at[pl.ds(there, cols), rows_at(first + ROWS), :],
            send_sem=pair_send.at[step],
            recv_sem=pair_recv.at[step],
            device_id={"lon": partner},
            device_id_type=MESH,
        )

    def fwd_copy(step):
        first = chunk_at(step) * ROWS + ROWS
        return pltpu.make_async_remote_copy(
            src_ref=ext.at[pl.ds(fwd_from, HALO), rows_at(first), :],
            dst_ref=ext.at[pl.ds(fwd_to, HALO), rows_at(first), :],
            send_sem=fwd_send.at[step],
            recv_sem=fwd_recv.at[step],
            device_id={"lon": onward},
            device_id_type=MESH,
        )

    edge = chunk_at(0) * ROWS
    edge_there = jnp.where(lat == 0, 0, rows + ROWS)

    def lat_copy(which, source, first, count, start):
        return pltpu.make_async_remote_copy(
            src_ref=source,
            dst_ref=ext.at[pl.ds(first, count), rows_at(edge_there), :],
            send_sem=lat_send.at[which],
            recv_sem=lat_recv.at[which],
            device_id={"lat": other},
            device_id_type=MESH,
        )

    lat_own = lat_copy(0, x_ref.at[:, rows_at(edge), :], cols, cols, edge)
    lat_pair = lat_copy(
        1, ext.at[pl.ds(here, cols), rows_at(edge + ROWS), :], here, cols, edge
    )
    lat_fwd = lat_copy(
        2, ext.at[pl.ds(fwd_to, HALO), rows_at(edge + ROWS), :], fwd_to, HALO, edge
    )

    pairs = [pair_copy(step) for step in range(chunks)]
    fwds = [fwd_copy(step) for step in range(chunks)]
    for copy in pairs:
        copy.start()
    lat_own.start()

    beyond = jnp.where(lat == 0, 0, rows + ROWS)
    ext[:, rows_at(beyond), :] = jnp.zeros((3 * cols, ROWS, width), ext.dtype)

    at = lax.broadcasted_iota(jnp.int32, (128, 256), 0)
    lane = lax.broadcasted_iota(jnp.int32, (128, 256), 1)
    same_col = (lane >> 4) == ((at >> 3) & 3) * BLOCK + (at >> 5)
    for row in range(8):
        same = same_col & ((lane & 15) == (((at & 7) + row - RAD) & 15))
        hot[row] = jnp.where(same, 1.0, 0.0).astype(jnp.bfloat16)

    slot = lax.broadcasted_iota(jnp.int32, (SLOTS, rows), 0)
    code = (cols_ref[...] - reach_ref[...] + 2) * 8 + rows_ref[...]
    code = jnp.where(slot < counts_ref[...], code, -1)
    place = lax.broadcasted_iota(jnp.int32, (32, rows), 0)
    row_of = lax.broadcasted_iota(jnp.int32, (rows, 256), 0)
    lane_of = lax.broadcasted_iota(jnp.int32, (rows, 256), 1)

    def build(k, carry):
        parts = []
        for t in range(BLOCK):
            values = filt_ref[k * BLOCK + t].astype(jnp.float32)
            total = jnp.zeros((32, rows), jnp.float32)
            for s in range(SLOTS):
                total += jnp.where(place == code[s : s + 1, :], values[s : s + 1, :], 0.0)
            parts.append(total)
        profile = jnp.concatenate(parts, axis=0).astype(jnp.bfloat16)
        result = jnp.zeros((rows, 256), jnp.float32)
        for row in range(8):
            spread = lax.dot_general(
                profile,
                hot[row],
                (((0,), (0,)), ((), ())),
                preferred_element_type=jnp.float32,
            )
            result = jnp.where((row_of & 7) == row, spread, result)
        turned = jnp.where(
            (lane_of & 15) < 8, pltpu.roll(result, 248, 1), pltpu.roll(result, 8, 1)
        )
        taps[k] = jnp.where((row_of & 8) == 8, turned, result)
        return carry

    lax.fori_loop(0, BASIS, build, 0)
    own_copy.wait()
    mix_copy.wait()

    low = cols - HALO
    span = cols + 2 * HALO - 1
    row16 = lax.broadcasted_iota(jnp.int32, (span, ROWS, width), 1)

    def compute(step):
        first = pl.multiple_of(chunk_at(step) * ROWS, ROWS)
        held = pl.ds(low, span)
        before = ext[held, pl.ds(first, ROWS), :].astype(jnp.float32)
        middle = ext[held, pl.ds(pl.multiple_of(first + ROWS, ROWS), ROWS), :].astype(jnp.float32)
        after = ext[held, pl.ds(pl.multiple_of(first + 2 * ROWS, ROWS), ROWS), :].astype(jnp.float32)
        near[...] = jnp.where(row16 < 12, middle, before).astype(jnp.bfloat16)
        far[...] = jnp.where(row16 < 4, after, middle).astype(jnp.bfloat16)
        tap = taps[:, pl.ds(first, ROWS), :]
        tap_near = tap[:, :8, :].reshape(BASIS * 8, 256).astype(jnp.bfloat16)
        tap_far = tap[:, 8:, :].reshape(BASIS * 8, 256).astype(jnp.bfloat16)
        for col in range(cols):
            sums = [
                jnp.dot(
                    tap_part,
                    source[col : col + 16].reshape(256, width),
                    preferred_element_type=jnp.float32,
                )
                for tap_part, source in ((tap_near, near), (tap_far, far))
            ]
            for k in range(BASIS):
                both = jnp.concatenate([part[8 * k : 8 * k + 8] for part in sums], axis=0)
                conv[col * ROWS : (col + 1) * ROWS, k * width : (k + 1) * width] = both.astype(
                    jnp.bfloat16
                )
        pre = jnp.dot(conv[...], mix[...], preferred_element_type=jnp.float32) + bias_ref[...]
        act = pre * (1.0 + lax.erf(pre * (0.5**0.5))) * 0.5
        out_ref[:, pl.ds(first, ROWS), :] = act.astype(jnp.bfloat16).reshape(cols, ROWS, width)

    for step in range(chunks):
        pairs[step].wait_recv()
        fwds[step].start()
        if step == 0:
            lat_pair.start()
            lat_own.wait_recv()
            fwds[0].wait_recv()
            lat_fwd.start()
            lat_pair.wait_recv()
            lat_fwd.wait_recv()
        else:
            fwds[step].wait_recv()
            compute(step - 1)
    compute(chunks - 1)
    for copy in pairs + fwds + [lat_own, lat_pair, lat_fwd]:
        copy.wait_send()


def body(lon_size, field, reach, slot_rows, slot_cols, counts, filters, mixing, bias):
    rows, cols, width = field.shape
    chunks = rows // ROWS
    vmem = pl.BlockSpec(memory_space=pltpu.VMEM)
    anywhere = pl.BlockSpec(memory_space=pl.ANY)
    dma = pltpu.SemaphoreType.DMA
    span = cols + 2 * HALO - 1
    out = pl.pallas_call(
        functools.partial(kernel, lon_size),
        out_shape=jax.ShapeDtypeStruct((cols, rows, width), jnp.bfloat16),
        in_specs=[anywhere, vmem, vmem, vmem, vmem, vmem, anywhere, vmem],
        out_specs=vmem,
        scratch_shapes=[
            pltpu.VMEM((3 * cols, rows + 2 * ROWS, width), jnp.bfloat16),
            pltpu.VMEM(mixing.shape, jnp.bfloat16),
            pltpu.VMEM((8, 128, 256), jnp.bfloat16),
            pltpu.VMEM((BASIS, rows, 256), jnp.float32),
            pltpu.VMEM((span, ROWS, width), jnp.bfloat16),
            pltpu.VMEM((span, ROWS, width), jnp.bfloat16),
            pltpu.VMEM((cols * ROWS, BASIS * width), jnp.bfloat16),
            dma,
            dma,
            dma((chunks,)),
            dma((chunks,)),
            dma((chunks,)),
            dma((chunks,)),
            dma((3,)),
            dma((3,)),
        ],
        compiler_params=pltpu.CompilerParams(
            collective_id=0, has_side_effects=True, vmem_limit_bytes=48 * 2**20
        ),
    )(
        field.transpose(1, 0, 2),
        slot_rows.T,
        slot_cols.T,
        reach[None, :],
        counts[None, :],
        filters.transpose(2, 1, 0),
        mixing,
        bias[None, :],
    )
    return out.transpose(1, 0, 2)


def solution(mesh):
    return jax.shard_map(
        functools.partial(body, mesh.shape["lon"]),
        mesh=mesh,
        in_specs=(
            P(("members", "lat"), "lon", None),
            P("lat"),
            P("lat", None),
            P("lat", None),
            P("lat"),
            P("lat", None, None),
            P(),
            P(),
        ),
        out_specs=P(("members", "lat"), "lon", None),
        check_vma=False,
    )
```

```python
import functools

import jax
import jax.numpy as jnp
from jax import lax
from jax.experimental import pallas as pl
from jax.experimental.pallas import tpu as pltpu
from jax.sharding import PartitionSpec as P

BASIS = 9
RAD = 3
BLOCK = 4
SLOTS = 16
HALO = 8
ROWS = 16
MESH = pl.DeviceIdType.MESH


def kernel(
    lon_size,
    x_ref,
    rows_in,
    cols_in,
    reach_in,
    counts_in,
    filt_in,
    mix_ref,
    bias_in,
    out_ref,
    ext,
    mix,
    rows_ref,
    cols_ref,
    reach_ref,
    counts_ref,
    filt_ref,
    bias_ref,
    hot,
    taps,
    near,
    far,
    conv,
    small_sem,
    own_sem,
    mix_sem,
    pair_send,
    pair_recv,
    fwd_send,
    fwd_recv,
    lat_send,
    lat_recv,
):
    cols, rows, width = x_ref.shape
    chunks = rows // ROWS
    lon = lax.axis_index("lon")
    lat = lax.axis_index("lat")
    even = lax.rem(lon, 2) == 0
    partner = jnp.where(even, lon + 1, lon - 1)
    ahead = lax.rem(lon + 2, lon_size)
    behind = lax.rem(lon + lon_size - 2, lon_size)
    onward = jnp.where(even, ahead, behind)
    other = 1 - lat

    def chunk_at(step):
        return jnp.where(lat == 0, chunks - 1 - step, step)

    def rows_at(start):
        return pl.ds(pl.multiple_of(start, ROWS), ROWS)

    own_copy = pltpu.make_async_copy(
        x_ref, ext.at[pl.ds(cols, cols), pl.ds(ROWS, rows), :], own_sem
    )
    own_copy.start()
    mix_copy = pltpu.make_async_copy(mix_ref, mix, mix_sem)
    mix_copy.start()
    small = [
        pltpu.make_async_copy(source, target, small_sem.at[index])
        for index, (source, target) in enumerate(
            (
                (rows_in, rows_ref),
                (cols_in, cols_ref),
                (reach_in, reach_ref),
                (counts_in, counts_ref),
                (filt_in, filt_ref),
                (bias_in, bias_ref),
            )
        )
    ]
    for copy in small:
        copy.start()

    barrier = pltpu.get_barrier_semaphore()
    for target in ({"lon": partner}, {"lon": ahead}, {"lon": behind}, {"lat": other}):
        pl.semaphore_signal(barrier, inc=1, device_id=target, device_id_type=MESH)
    pl.semaphore_wait(barrier, 4)

    there = jnp.where(even, 0, 2 * cols)
    here = 2 * cols - there
    fwd_from = jnp.where(even, here + cols - HALO, here)
    fwd_to = jnp.where(even, cols - HALO, 2 * cols)

    on_first = jnp.where(even, 0, cols - HALO)
    off_first = jnp.where(even, HALO, 0)

    def pair_copy(step, which, column, count):
        first = chunk_at(step) * ROWS
        return pltpu.make_async_remote_copy(
            src_ref=x_ref.at[pl.ds(column, count), rows_at(first), :],
            dst_ref=ext.at[pl.ds(there + column, count), rows_at(first + ROWS), :],
            send_sem=pair_send.at[which, step],
            recv_sem=pair_recv.at[which, step],
            device_id={"lon": partner},
            device_id_type=MESH,
        )

    def fwd_copy(step):
        first = chunk_at(step) * ROWS + ROWS
        return pltpu.make_async_remote_copy(
            src_ref=ext.at[pl.ds(fwd_from, HALO), rows_at(first), :],
            dst_ref=ext.at[pl.ds(fwd_to, HALO), rows_at(first), :],
            send_sem=fwd_send.at[step],
            recv_sem=fwd_recv.at[step],
            device_id={"lon": onward},
            device_id_type=MESH,
        )

    edge = chunk_at(0) * ROWS
    edge_there = jnp.where(lat == 0, 0, rows + ROWS)

    def lat_copy(which, source, first, count, start):
        return pltpu.make_async_remote_copy(
            src_ref=source,
            dst_ref=ext.at[pl.ds(first, count), rows_at(edge_there), :],
            send_sem=lat_send.at[which],
            recv_sem=lat_recv.at[which],
            device_id={"lat": other},
            device_id_type=MESH,
        )

    lat_own = lat_copy(0, x_ref.at[:, rows_at(edge), :], cols, cols, edge)
    lat_pair = lat_copy(
        1, ext.at[pl.ds(here, cols), rows_at(edge + ROWS), :], here, cols, edge
    )
    lat_fwd = lat_copy(
        2, ext.at[pl.ds(fwd_to, HALO), rows_at(edge + ROWS), :], fwd_to, HALO, edge
    )

    pairs = [pair_copy(step, 0, on_first, HALO) for step in range(chunks)]
    rests = [pair_copy(step, 1, off_first, cols - HALO) for step in range(chunks)]
    fwds = [fwd_copy(step) for step in range(chunks)]
    for copy in pairs + rests:
        copy.start()
    lat_own.start()

    beyond = jnp.where(lat == 0, 0, rows + ROWS)
    ext[:, rows_at(beyond), :] = jnp.zeros((3 * cols, ROWS, width), ext.dtype)

    at = lax.broadcasted_iota(jnp.int32, (128, 256), 0)
    lane = lax.broadcasted_iota(jnp.int32, (128, 256), 1)
    same_col = (lane >> 4) == ((at >> 3) & 3) * BLOCK + (at >> 5)
    for row in range(8):
        same = same_col & ((lane & 15) == (((at & 7) + row - RAD) & 15))
        hot[row] = jnp.where(same, 1.0, 0.0).astype(jnp.bfloat16)

    for copy in small:
        copy.wait()
    slot = lax.broadcasted_iota(jnp.int32, (SLOTS, rows), 0)
    code = (cols_ref[...] - reach_ref[...][None, :] + 2) * 8 + rows_ref[...]
    code = jnp.where(slot < counts_ref[...][None, :], code, -1)
    place = lax.broadcasted_iota(jnp.int32, (32, rows), 0)
    row_of = lax.broadcasted_iota(jnp.int32, (rows, 256), 0)
    lane_of = lax.broadcasted_iota(jnp.int32, (rows, 256), 1)

    def build(k, carry):
        parts = []
        for t in range(BLOCK):
            values = filt_ref[k * BLOCK + t].astype(jnp.float32)
            total = jnp.zeros((32, rows), jnp.float32)
            for s in range(SLOTS):
                total += jnp.where(place == code[s : s + 1, :], values[s : s + 1, :], 0.0)
            parts.append(total)
        profile = jnp.concatenate(parts, axis=0).astype(jnp.bfloat16)
        result = jnp.zeros((rows, 256), jnp.float32)
        for row in range(8):
            spread = lax.dot_general(
                profile,
                hot[row],
                (((0,), (0,)), ((), ())),
                preferred_element_type=jnp.float32,
            )
            result = jnp.where((row_of & 7) == row, spread, result)
        turned = jnp.where(
            (lane_of & 15) < 8, pltpu.roll(result, 248, 1), pltpu.roll(result, 8, 1)
        )
        taps[k] = jnp.where((row_of & 8) == 8, turned, result)
        return carry

    lax.fori_loop(0, BASIS, build, 0)
    own_copy.wait()
    mix_copy.wait()

    low = cols - HALO
    span = cols + 2 * HALO - 1
    row16 = lax.broadcasted_iota(jnp.int32, (span, ROWS, width), 1)

    def compute(step):
        first = pl.multiple_of(chunk_at(step) * ROWS, ROWS)
        held = pl.ds(low, span)
        before = ext[held, pl.ds(first, ROWS), :].astype(jnp.float32)
        middle = ext[held, pl.ds(pl.multiple_of(first + ROWS, ROWS), ROWS), :].astype(jnp.float32)
        after = ext[held, pl.ds(pl.multiple_of(first + 2 * ROWS, ROWS), ROWS), :].astype(jnp.float32)
        near[...] = jnp.where(row16 < 12, middle, before).astype(jnp.bfloat16)
        far[...] = jnp.where(row16 < 4, after, middle).astype(jnp.bfloat16)
        tap = taps[:, pl.ds(first, ROWS), :]
        tap_near = tap[:, :8, :].reshape(BASIS * 8, 256).astype(jnp.bfloat16)
        tap_far = tap[:, 8:, :].reshape(BASIS * 8, 256).astype(jnp.bfloat16)
        for col in range(cols):
            sums = [
                jnp.dot(
                    tap_part,
                    source[col : col + 16].reshape(256, width),
                    preferred_element_type=jnp.float32,
                )
                for tap_part, source in ((tap_near, near), (tap_far, far))
            ]
            for k in range(BASIS):
                both = jnp.concatenate([part[8 * k : 8 * k + 8] for part in sums], axis=0)
                conv[col * ROWS : (col + 1) * ROWS, k * width : (k + 1) * width] = both.astype(
                    jnp.bfloat16
                )
        pre = jnp.dot(conv[...], mix[...], preferred_element_type=jnp.float32) + bias_ref[...][None, :]
        act = pre * (1.0 + lax.erf(pre * (0.5**0.5))) * 0.5
        out_ref[:, pl.ds(first, ROWS), :] = act.astype(jnp.bfloat16).reshape(cols, ROWS, width)

    for step in range(chunks):
        pairs[step].wait_recv()
        fwds[step].start()
        if step == 1:
            fwds[0].wait_recv()
            lat_fwd.start()
    rests[0].wait_recv()
    lat_pair.start()
    for copy in (lat_own, lat_pair, lat_fwd):
        copy.wait_recv()
    for step in range(1, chunks):
        rests[step].wait_recv()
        fwds[step].wait_recv()
        compute(step - 1)
    compute(chunks - 1)
    for copy in pairs + rests + fwds + [lat_own, lat_pair, lat_fwd]:
        copy.wait_send()


def body(lon_size, field, reach, slot_rows, slot_cols, counts, filters, mixing, bias):
    rows, cols, width = field.shape
    chunks = rows // ROWS
    vmem = pl.BlockSpec(memory_space=pltpu.VMEM)
    anywhere = pl.BlockSpec(memory_space=pl.ANY)
    dma = pltpu.SemaphoreType.DMA
    span = cols + 2 * HALO - 1
    out = pl.pallas_call(
        functools.partial(kernel, lon_size),
        out_shape=jax.ShapeDtypeStruct((cols, rows, width), jnp.bfloat16),
        in_specs=[anywhere] * 8,
        out_specs=vmem,
        scratch_shapes=[
            pltpu.VMEM((3 * cols, rows + 2 * ROWS, width), jnp.bfloat16),
            pltpu.VMEM(mixing.shape, jnp.bfloat16),
            pltpu.VMEM((SLOTS, rows), jnp.int32),
            pltpu.VMEM((SLOTS, rows), jnp.int32),
            pltpu.VMEM((rows,), jnp.int32),
            pltpu.VMEM((rows,), jnp.int32),
            pltpu.VMEM((BASIS * BLOCK, SLOTS, rows), jnp.bfloat16),
            pltpu.VMEM((width,), jnp.float32),
            pltpu.VMEM((8, 128, 256), jnp.bfloat16),
            pltpu.VMEM((BASIS, rows, 256), jnp.float32),
            pltpu.VMEM((span, ROWS, width), jnp.bfloat16),
            pltpu.VMEM((span, ROWS, width), jnp.bfloat16),
            pltpu.VMEM((cols * ROWS, BASIS * width), jnp.bfloat16),
            dma((6,)),
            dma,
            dma,
            dma((2, chunks)),
            dma((2, chunks)),
            dma((chunks,)),
            dma((chunks,)),
            dma((3,)),
            dma((3,)),
        ],
        compiler_params=pltpu.CompilerParams(
            collective_id=0, has_side_effects=True, vmem_limit_bytes=60 * 2**20
        ),
    )(
        field.transpose(1, 0, 2),
        slot_rows.T,
        slot_cols.T,
        reach,
        counts,
        filters.transpose(2, 1, 0),
        mixing,
        bias,
    )
    return out.transpose(1, 0, 2)


def solution(mesh):
    return jax.shard_map(
        functools.partial(body, mesh.shape["lon"]),
        mesh=mesh,
        in_specs=(
            P(("members", "lat"), "lon", None),
            P("lat"),
            P("lat", None),
            P("lat", None),
            P("lat"),
            P("lat", None, None),
            P(),
            P(),
        ),
        out_specs=P(("members", "lat"), "lon", None),
        check_vma=False,
    )
```

```python
import functools

import jax
import jax.numpy as jnp
from jax import lax
from jax.experimental import pallas as pl
from jax.experimental.pallas import tpu as pltpu
from jax.sharding import PartitionSpec as P

BASIS = 9
RAD = 3
BLOCK = 4
SLOTS = 16
HALO = 8
ROWS = 16
MESH = pl.DeviceIdType.MESH


def kernel(
    lon_size,
    x_ref,
    rows_in,
    cols_in,
    reach_in,
    counts_in,
    filt_in,
    mix_ref,
    bias_in,
    out_ref,
    ext,
    mix,
    rows_ref,
    cols_ref,
    reach_ref,
    counts_ref,
    filt_ref,
    bias_ref,
    hot,
    taps,
    near,
    far,
    conv,
    small_sem,
    own_sem,
    mix_sem,
    pair_send,
    pair_recv,
    fwd_send,
    fwd_recv,
    lat_send,
    lat_recv,
):
    cols, rows, width = x_ref.shape
    chunks = rows // ROWS
    lon = lax.axis_index("lon")
    lat = lax.axis_index("lat")
    even = lax.rem(lon, 2) == 0
    partner = jnp.where(even, lon + 1, lon - 1)
    ahead = lax.rem(lon + 2, lon_size)
    behind = lax.rem(lon + lon_size - 2, lon_size)
    onward = jnp.where(even, ahead, behind)
    other = 1 - lat

    def chunk_at(step):
        return jnp.where(lat == 0, chunks - 1 - step, step)

    def rows_at(start):
        return pl.ds(pl.multiple_of(start, ROWS), ROWS)

    barrier = pltpu.get_barrier_semaphore()
    for target in ({"lon": partner}, {"lon": ahead}, {"lon": behind}, {"lat": other}):
        pl.semaphore_signal(barrier, inc=1, device_id=target, device_id_type=MESH)

    own_copy = pltpu.make_async_copy(
        x_ref, ext.at[pl.ds(cols, cols), pl.ds(ROWS, rows), :], own_sem
    )
    own_copy.start()
    mix_copy = pltpu.make_async_copy(mix_ref, mix, mix_sem)
    mix_copy.start()
    small = [
        pltpu.make_async_copy(source, target, small_sem.at[index])
        for index, (source, target) in enumerate(
            (
                (rows_in, rows_ref),
                (cols_in, cols_ref),
                (reach_in, reach_ref),
                (counts_in, counts_ref),
                (filt_in, filt_ref),
                (bias_in, bias_ref),
            )
        )
    ]
    for copy in small:
        copy.start()

    pl.semaphore_wait(barrier, 4)

    there = jnp.where(even, 0, 2 * cols)
    here = 2 * cols - there
    fwd_from = jnp.where(even, here + cols - HALO, here)
    fwd_to = jnp.where(even, cols - HALO, 2 * cols)

    on_first = jnp.where(even, 0, cols - HALO)
    off_first = jnp.where(even, HALO, 0)

    def pair_copy(step, which, column, count):
        first = chunk_at(step) * ROWS
        return pltpu.make_async_remote_copy(
            src_ref=x_ref.at[pl.ds(column, count), rows_at(first), :],
            dst_ref=ext.at[pl.ds(there + column, count), rows_at(first + ROWS), :],
            send_sem=pair_send.at[which, step],
            recv_sem=pair_recv.at[which, step],
            device_id={"lon": partner},
            device_id_type=MESH,
        )

    def fwd_copy(step):
        first = chunk_at(step) * ROWS + ROWS
        return pltpu.make_async_remote_copy(
            src_ref=ext.at[pl.ds(fwd_from, HALO), rows_at(first), :],
            dst_ref=ext.at[pl.ds(fwd_to, HALO), rows_at(first), :],
            send_sem=fwd_send.at[step],
            recv_sem=fwd_recv.at[step],
            device_id={"lon": onward},
            device_id_type=MESH,
        )

    edge = chunk_at(0) * ROWS
    edge_there = jnp.where(lat == 0, 0, rows + ROWS)

    def lat_copy(which, source, first, count, start):
        return pltpu.make_async_remote_copy(
            src_ref=source,
            dst_ref=ext.at[pl.ds(first, count), rows_at(edge_there), :],
            send_sem=lat_send.at[which],
            recv_sem=lat_recv.at[which],
            device_id={"lat": other},
            device_id_type=MESH,
        )

    lat_own = lat_copy(0, x_ref.at[:, rows_at(edge), :], cols, cols, edge)
    lat_pair = lat_copy(
        1, ext.at[pl.ds(here, cols), rows_at(edge + ROWS), :], here, cols, edge
    )
    lat_fwd = lat_copy(
        2, ext.at[pl.ds(fwd_to, HALO), rows_at(edge + ROWS), :], fwd_to, HALO, edge
    )

    pairs = [pair_copy(step, 0, on_first, HALO) for step in range(chunks)]
    rests = [pair_copy(step, 1, off_first, cols - HALO) for step in range(chunks)]
    fwds = [fwd_copy(step) for step in range(chunks)]
    for copy in pairs + rests:
        copy.start()
    lat_own.start()

    beyond = jnp.where(lat == 0, 0, rows + ROWS)
    ext[:, rows_at(beyond), :] = jnp.zeros((3 * cols, ROWS, width), ext.dtype)

    at = lax.broadcasted_iota(jnp.int32, (128, 256), 0)
    lane = lax.broadcasted_iota(jnp.int32, (128, 256), 1)
    same_col = (lane >> 4) == ((at >> 3) & 3) * BLOCK + (at >> 5)
    for row in range(8):
        same = same_col & ((lane & 15) == (((at & 7) + row - RAD) & 15))
        hot[row] = jnp.where(same, 1.0, 0.0).astype(jnp.bfloat16)

    for copy in small:
        copy.wait()
    slot = lax.broadcasted_iota(jnp.int32, (SLOTS, rows), 0)
    code = (cols_ref[...] - reach_ref[...][None, :] + 2) * 8 + rows_ref[...]
    code = jnp.where(slot < counts_ref[...][None, :], code, -1)
    place = lax.broadcasted_iota(jnp.int32, (32, rows), 0)
    row_of = lax.broadcasted_iota(jnp.int32, (rows, 256), 0)
    lane_of = lax.broadcasted_iota(jnp.int32, (rows, 256), 1)

    def build(k, carry):
        parts = []
        for t in range(BLOCK):
            values = filt_ref[k * BLOCK + t].astype(jnp.float32)
            total = jnp.zeros((32, rows), jnp.float32)
            for s in range(SLOTS):
                total += jnp.where(place == code[s : s + 1, :], values[s : s + 1, :], 0.0)
            parts.append(total)
        profile = jnp.concatenate(parts, axis=0).astype(jnp.bfloat16)
        result = jnp.zeros((rows, 256), jnp.float32)
        for row in range(8):
            spread = lax.dot_general(
                profile,
                hot[row],
                (((0,), (0,)), ((), ())),
                preferred_element_type=jnp.float32,
            )
            result = jnp.where((row_of & 7) == row, spread, result)
        turned = jnp.where(
            (lane_of & 15) < 8, pltpu.roll(result, 248, 1), pltpu.roll(result, 8, 1)
        )
        taps[k] = jnp.where((row_of & 8) == 8, turned, result)
        return carry

    lax.fori_loop(0, BASIS, build, 0)
    own_copy.wait()
    mix_copy.wait()

    low = cols - HALO
    span = cols + 2 * HALO - 1
    row16 = lax.broadcasted_iota(jnp.int32, (span, ROWS, width), 1)

    def compute(step):
        first = pl.multiple_of(chunk_at(step) * ROWS, ROWS)
        held = pl.ds(low, span)
        before = ext[held, pl.ds(first, ROWS), :].astype(jnp.float32)
        middle = ext[held, pl.ds(pl.multiple_of(first + ROWS, ROWS), ROWS), :].astype(jnp.float32)
        after = ext[held, pl.ds(pl.multiple_of(first + 2 * ROWS, ROWS), ROWS), :].astype(jnp.float32)
        near[...] = jnp.where(row16 < 12, middle, before).astype(jnp.bfloat16)
        far[...] = jnp.where(row16 < 4, after, middle).astype(jnp.bfloat16)
        tap = taps[:, pl.ds(first, ROWS), :]
        tap_near = tap[:, :8, :].reshape(BASIS * 8, 256).astype(jnp.bfloat16)
        tap_far = tap[:, 8:, :].reshape(BASIS * 8, 256).astype(jnp.bfloat16)
        for col in range(cols):
            sums = [
                jnp.dot(
                    tap_part,
                    source[col : col + 16].reshape(256, width),
                    preferred_element_type=jnp.float32,
                )
                for tap_part, source in ((tap_near, near), (tap_far, far))
            ]
            for k in range(BASIS):
                both = jnp.concatenate([part[8 * k : 8 * k + 8] for part in sums], axis=0)
                conv[col * ROWS : (col + 1) * ROWS, k * width : (k + 1) * width] = both.astype(
                    jnp.bfloat16
                )
        pre = jnp.dot(conv[...], mix[...], preferred_element_type=jnp.float32) + bias_ref[...][None, :]
        act = pre * (1.0 + lax.erf(pre * (0.5**0.5))) * 0.5
        out_ref[:, pl.ds(first, ROWS), :] = act.astype(jnp.bfloat16).reshape(cols, ROWS, width)

    for step in range(chunks):
        pairs[step].wait_recv()
        fwds[step].start()
        if step == 2:
            fwds[0].wait_recv()
            lat_fwd.start()
    rests[0].wait_recv()
    lat_pair.start()
    for copy in (lat_own, lat_pair, lat_fwd):
        copy.wait_recv()
    for step in range(1, chunks):
        rests[step].wait_recv()
        fwds[step].wait_recv()
        compute(step - 1)
    compute(chunks - 1)
    for copy in pairs + rests + fwds + [lat_own, lat_pair, lat_fwd]:
        copy.wait_send()


def body(lon_size, field, reach, slot_rows, slot_cols, counts, filters, mixing, bias):
    rows, cols, width = field.shape
    chunks = rows // ROWS
    vmem = pl.BlockSpec(memory_space=pltpu.VMEM)
    anywhere = pl.BlockSpec(memory_space=pl.ANY)
    dma = pltpu.SemaphoreType.DMA
    span = cols + 2 * HALO - 1
    out = pl.pallas_call(
        functools.partial(kernel, lon_size),
        out_shape=jax.ShapeDtypeStruct((cols, rows, width), jnp.bfloat16),
        in_specs=[anywhere] * 8,
        out_specs=vmem,
        scratch_shapes=[
            pltpu.VMEM((3 * cols, rows + 2 * ROWS, width), jnp.bfloat16),
            pltpu.VMEM(mixing.shape, jnp.bfloat16),
            pltpu.VMEM((SLOTS, rows), jnp.int32),
            pltpu.VMEM((SLOTS, rows), jnp.int32),
            pltpu.VMEM((rows,), jnp.int32),
            pltpu.VMEM((rows,), jnp.int32),
            pltpu.VMEM((BASIS * BLOCK, SLOTS, rows), jnp.bfloat16),
            pltpu.VMEM((width,), jnp.float32),
            pltpu.VMEM((8, 128, 256), jnp.bfloat16),
            pltpu.VMEM((BASIS, rows, 256), jnp.float32),
            pltpu.VMEM((span, ROWS, width), jnp.bfloat16),
            pltpu.VMEM((span, ROWS, width), jnp.bfloat16),
            pltpu.VMEM((cols * ROWS, BASIS * width), jnp.bfloat16),
            dma((6,)),
            dma,
            dma,
            dma((2, chunks)),
            dma((2, chunks)),
            dma((chunks,)),
            dma((chunks,)),
            dma((3,)),
            dma((3,)),
        ],
        compiler_params=pltpu.CompilerParams(
            collective_id=0, has_side_effects=True, vmem_limit_bytes=60 * 2**20
        ),
    )(
        field.transpose(1, 0, 2),
        slot_rows.T,
        slot_cols.T,
        reach,
        counts,
        filters.transpose(2, 1, 0),
        mixing,
        bias,
    )
    return out.transpose(1, 0, 2)


def solution(mesh):
    return jax.shard_map(
        functools.partial(body, mesh.shape["lon"]),
        mesh=mesh,
        in_specs=(
            P(("members", "lat"), "lon", None),
            P("lat"),
            P("lat", None),
            P("lat", None),
            P("lat"),
            P("lat", None, None),
            P(),
            P(),
        ),
        out_specs=P(("members", "lat"), "lon", None),
        check_vma=False,
    )
```
